128 devices in a mesh: state: 8 (over x, core), vocab: 16 (over z, y).
Axes of the slice: x: 4, y: 4, z: 4, core: 2. Of those that a mesh axis runs over, the one named last changes fastest.
Arguments:
- state_emb: bfloat16 [8192, 512], P('state', 'vocab'), may hold values from -11 to 11
- tok_emb: bfloat16 [77824, 512], P('vocab', 'state'), may hold values from -0.70710678 to 0.70710678
- counts: bfloat16 [8192, 77824], P('state', 'vocab'), may hold values from 0 to 0.6
Outputs:
- grad_state: bfloat16 [8192, 512], P('state', 'vocab')
- grad_tok: bfloat16 [77824, 512], P('vocab', 'state')
The draws below stay inside these ranges and needn't reach their ends.
All inputs are finite; a program needn't handle non-finite values.
Results may differ from the reference program's by a relative error of at most 0.02.
Values may be sent and summed in bfloat16 or wider, within the bound.
No kernel may reach another device: no remote copies, remote signals or barrier semaphores. Data moves between devices by JAX's collectives and lax.ppermute only.
A program may use at most 128 MiB of HBM per device.

```python
import jax
import jax.numpy as jnp
from jax import lax

E = 512
V_DEV = 4864
S_DEV = 1024
S = 8192
V = 77824
N_VOCAB = 16


def common_direction(key):
    return jax.random.uniform(jax.random.fold_in(key, 5), (E,), jnp.float32, -1.7, 1.7)


def picked_rows():
    return (jnp.arange(S) % 1021 == 0)[:, None]


def draw_state_emb(key, part):
    direction = common_direction(key)
    key = jax.random.fold_in(key, 11)
    first_key = jax.random.fold_in(key, 0)
    third_key = jax.random.fold_in(key, 2)
    strength = jax.random.uniform(third_key, (S, 1), jnp.float32, 2.0, 6.0)
    strength = jnp.where((jnp.arange(S) == 0)[:, None], 6.0, strength)
    picked = picked_rows()
    drawn = jnp.clip(jax.random.normal(first_key, (S, E), jnp.float32), -4.0, 4.0) * 0.5
    values = jnp.where(picked, strength * direction[None, :], drawn)
    return values.astype(jnp.bfloat16)


def draw_tok_emb(key, part):
    direction = common_direction(key)
    key = jax.random.fold_in(key, 12)
    first_key = jax.random.fold_in(key, 0)
    third_key = jax.random.fold_in(key, 2)
    factor = 3.0 / jnp.sqrt(jnp.float32(E))
    offset = jax.random.uniform(third_key, (), jnp.float32, 0.015, 0.025)
    index = jnp.arange(V)
    strength = jnp.where(index == V - 1, 2.0, 2.0 + offset)[:, None]
    special = strength * 26.0 * direction[None, :] / jnp.float32(E)
    picked = (index >= V - 2)[:, None]
    drawn = jnp.clip(jax.random.normal(first_key, (V, E), jnp.float32), -4.0, 4.0) * factor
    values = jnp.where(picked, special, drawn)
    return values.astype(jnp.bfloat16)


def draw_counts(key, part):
    key = jax.random.fold_in(key, 13)
    first_key, second_key = jax.random.split(key, 2)
    base = jax.random.uniform(first_key, (S, V), jnp.float32)
    row_scale = jnp.exp(jax.random.uniform(second_key, (S, 1), jnp.float32, jnp.log(0.2), jnp.log(2.0)))
    row_scale = jnp.where(picked_rows(), row_scale * 0.002, row_scale)
    ramp = 1.0 + 2.0 * jnp.arange(V, dtype=jnp.float32)[None, :] / (V - 1)
    return (0.03 * base * row_scale * ramp).astype(jnp.bfloat16)


def setup_inputs(seed: int = 0) -> dict:
    seeds = jax.random.split(jax.random.key(seed), 4)
    return {
        "state_emb": draw_state_emb(jax.random.fold_in(seeds[3], 71), 0),
        "tok_emb": draw_tok_emb(jax.random.fold_in(seeds[3], 71), 0),
        "counts": draw_counts(jax.random.fold_in(seeds[3], 71), 0),
    }


def reference(state_emb, tok_emb, counts):
    rows = S_DEV
    tok_blocks = tok_emb.astype(jnp.float32).reshape(N_VOCAB, V_DEV, E)

    def block_step(token_acc, block_index):
        begin_row = block_index * rows
        state_block = lax.dynamic_slice_in_dim(state_emb, begin_row, rows, 0)
        count_block = lax.dynamic_slice_in_dim(counts, begin_row, rows, 0)
        logits = jnp.dot(state_block, tok_emb.T, preferred_element_type=jnp.float32)
        row_top = jnp.max(logits, axis=1, keepdims=True)
        weights = jnp.exp(logits - row_top)
        row_total = jnp.sum(weights, axis=1, keepdims=True)
        wide_counts = count_block.astype(jnp.float32)
        row_counts = jnp.sum(wide_counts, axis=1, keepdims=True)
        dlogits = (wide_counts - weights / row_total * row_counts).astype(jnp.bfloat16)
        split_grads = dlogits.astype(jnp.float32).reshape(rows, N_VOCAB, V_DEV)
        state_terms = jnp.einsum("rnv,nve->nre", split_grads, tok_blocks).astype(jnp.bfloat16)
        state_terms = lax.optimization_barrier(state_terms)
        state_grad = jnp.sum(state_terms.astype(jnp.float32), axis=0).astype(jnp.bfloat16)
        tok_term = jnp.dot(dlogits.T, state_block, preferred_element_type=jnp.float32).astype(jnp.bfloat16)
        tok_term = lax.optimization_barrier(tok_term)
        token_acc = token_acc + tok_term.astype(jnp.float32)
        return token_acc, state_grad

    start_acc = jnp.zeros((V, E), jnp.float32)
    token_acc, state_grads = lax.scan(block_step, start_acc, jnp.arange(S // rows, dtype=jnp.int32))
    grad_state = state_grads.reshape(S, E)
    grad_tok = token_acc.astype(jnp.bfloat16)
    return grad_state, grad_tok
```

```python
import jax
import jax.numpy as jnp
from jax import lax
from jax.experimental import pallas as pl
from jax.experimental.pallas import tpu as pltpu
from jax.sharding import PartitionSpec as P

F32 = jnp.float32
BF16 = jnp.bfloat16
VMEM = pltpu.MemorySpace.VMEM
SMEM = pltpu.MemorySpace.SMEM

E = 512
ROWS = 1024
COLS = 4864
CHUNKS = ((0, 2560), (2560, 2304))
TILE = 256
NX, NY, NZ = 4, 4, 4


def core_swap(a):
    return lax.ppermute(a, "state", [(i, i ^ 1) for i in range(8)])


def x_shift(a, step):
    return lax.ppermute(a, "state", [(i, (i + 2 * step) % 8) for i in range(8)])


def shift(a, stage, step):
    perm = []
    for i in range(8):
        for j in range(16):
            z, y = divmod(j, NY)
            if (i % 2 + stage) % 2 == 0:
                y = (y + step) % NY
            else:
                z = (z + step) % NZ
            perm.append((i * 16 + j, i * 16 + z * NY + y))
    return lax.ppermute(a, ("state", "vocab"), perm)


def run(kernel, outs, *ins, flops=0, smem=0, limit=8, **kw):
    vmem = pl.BlockSpec(memory_space=VMEM)
    specs = [pl.BlockSpec(memory_space=SMEM)] * smem + [vmem] * (len(ins) - smem)
    args = list(ins[:smem]) + [pltpu.with_memory_space_constraint(a, VMEM) for a in ins[smem:]]
    moved = sum(a.size * a.dtype.itemsize for a in ins)
    return pl.pallas_call(
        kernel,
        out_shape=tuple(VMEM(shape, dtype) for shape, dtype in outs),
        in_specs=specs,
        out_specs=tuple([vmem] * len(outs)),
        compiler_params=pltpu.CompilerParams(vmem_limit_bytes=limit * 2**20),
        cost_estimate=pl.CostEstimate(flops=flops, bytes_accessed=moved, transcendentals=0),
        **kw,
    )(*args)


def eye():
    rows = lax.broadcasted_iota(jnp.int32, (128, 128), 0)
    return rows == lax.broadcasted_iota(jnp.int32, (128, 128), 1)


def to_lanes(column):
    return jnp.sum(jnp.where(eye(), jnp.broadcast_to(column, (128, 128)), 0.0), axis=0, keepdims=True)


def to_column(lanes):
    return jnp.sum(jnp.where(eye(), jnp.broadcast_to(lanes, (128, 128)), 0.0), axis=1, keepdims=True)


def assemble_kernel(off, s0, s1, s2, s3, b1, b2, b3, wide, tall):
    def put(slot, rows):
        wide[pl.ds(pl.multiple_of(off[slot], 32), 32), :] = rows

    for k, part in enumerate((s0, s1, s2, s3)):
        put(k, part[...])
    for g, part in enumerate((b1, b2, b3)):
        for k in range(4):
            put(4 * (g + 1) + k, part[32 * k : 32 * k + 32, :])
    tall[...] = wide[...].T


def softmax_kernel(s, *refs):
    parts, (w, stats, tokens), top = refs[:8], refs[8:11], refs[11]
    cols = w.shape[1]
    top[...] = jnp.full(top.shape, -jnp.inf, F32)

    def logits(i, carry):
        at = pl.ds(pl.multiple_of(i * TILE, TILE), TILE)
        tile = jnp.concatenate([p[:, at] for p in parts], axis=0)
        tokens[:, at] = tile
        out = jnp.dot(s[...], tile, preferred_element_type=F32)
        w[:, at] = out
        top[...] = jnp.maximum(top[...], jnp.maximum(out[:, :128], out[:, 128:]))
        return carry

    lax.fori_loop(0, cols // TILE, logits, 0)

    def block(r, carry):
        rows = pl.ds(pl.multiple_of(r * 128, 128), 128)
        row_top = jnp.max(top[rows, :], axis=1, keepdims=True)
        wide_top = jnp.broadcast_to(row_top, (128, 128))

        def weigh(i, acc):
            at = pl.ds(pl.multiple_of(i * 128, 128), 128)
            e = jnp.exp(w[rows, at] - wide_top)
            w[rows, at] = e
            return acc + e

        acc = lax.fori_loop(0, cols // 128, weigh, jnp.zeros((128, 128), F32), unroll=2)
        stats[pl.ds(r, 1), :] = to_lanes(row_top)
        stats[pl.ds(r + 8, 1), :] = to_lanes(jnp.sum(acc, axis=1, keepdims=True))
        return carry

    lax.fori_loop(0, ROWS // 128, block, 0)


def dlogits_kernel(w, counts, factor, s, dl, out):
    f = jnp.concatenate([to_column(factor[r : r + 1, :]) for r in range(ROWS // 128)], axis=0)

    def step(i, carry):
        at = pl.ds(pl.multiple_of(i * TILE, TILE), TILE)
        d = (counts[:, at].astype(F32) - w[:, at] * f).astype(BF16)
        dl[:, at] = d
        out[:, at] = jnp.dot(s[...], d, preferred_element_type=F32).astype(BF16)
        return carry

    lax.fori_loop(0, w.shape[1] // TILE, step, 0)


def tok_kernel(s, dl_a, dl_b, out):
    for dl, (first, width) in zip((dl_a, dl_b), CHUNKS):

        def step(i, carry):
            at = pl.ds(pl.multiple_of(i * TILE, TILE), TILE)
            to = pl.ds(pl.multiple_of(first + i * TILE, TILE), TILE)
            out[:, to] = jnp.dot(s[...], dl[:, at], preferred_element_type=F32).astype(BF16)
            return carry

        lax.fori_loop(0, width // TILE, step, 0)


def state_kernel(off, t_a, t_b, dl_a, dl_b, out, acc):
    dims = (((1,), (1,)), ((), ()))
    for q in range(4):
        rows = slice(256 * q, 256 * q + 256)
        acc[...] = lax.dot_general(t_a[...], dl_a[rows, :], dims, preferred_element_type=F32)
        acc[...] += lax.dot_general(t_b[...], dl_b[rows, :], dims, preferred_element_type=F32)
        for r in range(16):
            part = acc[pl.ds(pl.multiple_of(off[r], 32), 32), :]
            out[32 * r : 32 * r + 32, rows] = part.astype(BF16)


def combine(parts):
    tops = [p[:8] for p in parts]
    top = tops[0]
    for t in tops[1:]:
        top = jnp.maximum(top, t)
    total = sum(p[8:16] * jnp.exp(t - top) for p, t in zip(parts, tops))
    return jnp.concatenate([top, total, sum(p[16:] for p in parts)], axis=0)


def row_offsets():
    i, j = lax.axis_index("state"), lax.axis_index("vocab")
    x, c = i // 2, i % 2
    z, y = j // NY, j % NY
    slot = jnp.arange(16, dtype=jnp.int32)
    a, b = slot % 4, slot // 4
    from_y = jnp.where(c == 0, (y - a) % 4, (y - b) % 4)
    from_z = jnp.where(c == 0, (z - b) % 4, (z - a) % 4)
    k = from_z * NY + from_y
    owner = k // 2
    ahead = (owner // 2 - x) % 4
    place = jnp.where(ahead == 0, 0, jnp.where(ahead == 3, 1, jnp.where(ahead == 1, 2, 3)))
    return 128 * place + 64 * (owner % 2 != c) + 32 * (k % 2)


def add(*parts):
    return sum(p.astype(F32) for p in parts).astype(BF16)


def body(state_emb, tok_emb, counts):
    own = tok_emb.T
    s0 = state_emb.T
    off = row_offsets().astype(jnp.int32)

    halves = []
    for first, width in CHUNKS:
        t0 = own[:, first : first + width]
        halves.append((t0, x_shift(t0, 1), x_shift(t0, -1)))
    chunks = []
    for t0, t2, t4 in halves:
        far = jnp.concatenate([x_shift(t2[:32], 1), x_shift(t4[32:], -1)], axis=0)
        near = [t0, core_swap(t0), t2, core_swap(t2), t4, core_swap(t4), far, core_swap(far)]
        chunks.append(near)

    first_parts = [s0] + [shift(s0, 0, k) for k in (1, 2, 3)]
    block = jnp.concatenate(first_parts, axis=0)
    later = [shift(block, 1, k) for k in (1, 2, 3)]
    wide, tall = run(
        assemble_kernel, [((E, ROWS), BF16), ((ROWS, E), BF16)], off, *first_parts, *later, smem=1
    )

    row_counts = jnp.sum(counts, axis=1, dtype=F32).reshape(8, 128)

    weights, stats, tokens = [], [], []
    for parts, (first, width) in zip(chunks, CHUNKS):
        w, st, tk = run(
            softmax_kernel,
            [((ROWS, width), F32), ((16, 128), F32), ((E, width), BF16)],
            tall,
            *parts,
            flops=2 * ROWS * E * width,
            scratch_shapes=[pltpu.VMEM((ROWS, 128), F32)],
        )
        weights.append(w)
        stats.append(st)
        tokens.append(tk)

    none = jnp.zeros((8, 128), F32)
    total = combine(
        [jnp.concatenate([stats[0], row_counts], axis=0), jnp.concatenate([stats[1], none], axis=0)]
    )
    for stage in range(2):
        total = combine([total] + [shift(total, stage, k) for k in (1, 2, 3)])
    scale = total[16:] / total[8:16]

    dls, far_parts = [], []
    for w, st, (first, width) in zip(weights, stats, CHUNKS):
        factor = jnp.exp(st[:8] - total[:8]) * scale
        dl, part = run(
            dlogits_kernel,
            [((ROWS, width), BF16), ((128, width), BF16)],
            w,
            counts[:, first : first + width],
            factor,
            wide[384:],
            flops=2 * ROWS * 128 * width,
        )
        dls.append(dl)
        far_parts.append(part)
    far = jnp.concatenate(far_parts, axis=1)

    w6 = add(far[:64], core_swap(far[64:]))
    got_low = x_shift(w6[:32], 1)
    got_high = x_shift(w6[32:], -1)
    (mid,) = run(tok_kernel, [((256, COLS), BF16)], wide[128:384], *dls, flops=2 * ROWS * 256 * COLS)
    w2 = add(mid[:64], core_swap(mid[64:128]))
    w4 = add(mid[128:192], core_swap(mid[192:]))
    up_high = x_shift(w4[32:], 1)
    down_low = x_shift(w2[:32], -1)
    up_low = x_shift(add(w4[:32], got_low), 1)
    down_high = x_shift(add(w2[32:], got_high), -1)
    (near,) = run(tok_kernel, [((128, COLS), BF16)], wide[:128], *dls, flops=2 * ROWS * 128 * COLS)
    swapped = core_swap(near[64:])
    grad_tok = jnp.concatenate(
        [add(near[:32], swapped[:32], up_low, down_low), add(near[32:64], swapped[32:], up_high, down_high)],
        axis=0,
    )

    (g,) = run(
        state_kernel,
        [((E, ROWS), BF16)],
        off,
        *tokens,
        *dls,
        smem=1,
        flops=2 * ROWS * E * COLS,
        scratch_shapes=[pltpu.VMEM((E, 256), F32)],
    )
    g = add(g[:128], *[shift(g[128 * k : 128 * k + 128], 1, -k) for k in (1, 2, 3)])
    grad_state = add(g[:32], *[shift(g[32 * k : 32 * k + 32], 0, -k) for k in (1, 2, 3)])
    return grad_state.T, grad_tok.T


def solution(mesh):
    return jax.shard_map(
        body,
        mesh=mesh,
        in_specs=(P("state", "vocab"), P("vocab", "state"), P("state", "vocab")),
        out_specs=(P("state", "vocab"), P("vocab", "state")),
        check_vma=False,
    )
```

```python
import functools

import jax
import jax.numpy as jnp
from jax import lax
from jax.experimental import pallas as pl
from jax.experimental.pallas import tpu as pltpu
from jax.sharding import PartitionSpec as P

F32 = jnp.float32
BF16 = jnp.bfloat16
VMEM = pltpu.MemorySpace.VMEM
SMEM = pltpu.MemorySpace.SMEM
HBM = pltpu.MemorySpace.HBM

E = 512
ROWS = 1024
COLS = 4864
HALF = COLS // 2
HALVES = (slice(0, HALF), slice(HALF, COLS))
NX, NY, NZ = 4, 4, 4
GATHER = 2**31


def core_swap(a):
    return lax.ppermute(a, "state", [(i, i ^ 1) for i in range(8)])


def x_shift(a, step):
    return lax.ppermute(a, "state", [(i, (i + 2 * step) % 8) for i in range(8)])


def shift(a, stage, step):
    perm = []
    for i in range(8):
        for j in range(16):
            z, y = divmod(j, NY)
            if (i % 2 + stage) % 2 == 0:
                y = (y + step) % NY
            else:
                z = (z + step) % NZ
            perm.append((i * 16 + j, i * 16 + z * NY + y))
    return lax.ppermute(a, ("state", "vocab"), perm)


def run(kernel, outs, *ins, flops=64, smem=0, hbm=0, wait=(), limit=8, **kw):
    plain = smem + hbm
    vmem = pl.BlockSpec(memory_space=VMEM)
    anywhere = pl.BlockSpec(memory_space=pl.ANY)
    specs = [pl.BlockSpec(memory_space=SMEM)] * smem + [pl.BlockSpec(memory_space=HBM)] * hbm + [vmem] * (len(ins) - plain)
    args = list(ins[:smem]) + [pltpu.with_memory_space_constraint(a, HBM) for a in ins[smem:plain]]
    args += [pltpu.with_memory_space_constraint(a, VMEM) for a in ins[plain:]]

    def wrapped(*refs):
        kernel(*refs[: len(ins)], *refs[len(ins) + len(wait) :])

    return pl.pallas_call(
        wrapped,
        out_shape=tuple((space[0] if space else VMEM)(shape, dtype) for shape, dtype, *space in outs),
        in_specs=specs + [anywhere] * len(wait),
        out_specs=tuple(pl.BlockSpec(memory_space=o[2]) if o[2:] else vmem for o in outs),
        compiler_params=pltpu.CompilerParams(vmem_limit_bytes=limit * 2**20),
        cost_estimate=pl.CostEstimate(flops=flops, bytes_accessed=64, transcendentals=0),
        **kw,
    )(*args, *wait)


def eye():
    rows = lax.broadcasted_iota(jnp.int32, (128, 128), 0)
    return rows == lax.broadcasted_iota(jnp.int32, (128, 128), 1)


def to_lanes(column):
    return jnp.sum(jnp.where(eye(), jnp.broadcast_to(column, (128, 128)), 0.0), axis=0, keepdims=True)


def to_column(lanes):
    return jnp.sum(jnp.where(eye(), jnp.broadcast_to(lanes, (128, 128)), 0.0), axis=1, keepdims=True)


def hold_kernel(*refs):
    for a, out in zip(refs[:2], refs[2:]):
        out[...] = a[...]


def row_offset(slot):
    i, j = lax.axis_index("state"), lax.axis_index("vocab")
    x, c = lax.div(i, 2), lax.rem(i, 2)
    z, y = lax.div(j, NY), lax.rem(j, NY)
    b, a = divmod(slot, 4)
    y = lax.rem(y + 4 - jnp.where(c == 0, a, b), 4)
    z = lax.rem(z + 4 - jnp.where(c == 0, b, a), 4)
    k = z * NY + y
    owner = lax.div(k, 2)
    ahead = lax.rem(lax.div(owner, 2) + 4 - x, 4)
    place = jnp.where(ahead == 0, 0, jnp.where(ahead == 3, 1, jnp.where(ahead == 1, 2, 3)))
    other = jnp.where(lax.rem(owner, 2) == c, 0, 64)
    return pl.multiple_of(128 * place + other + 32 * lax.rem(k, 2), 32)


def assemble_kernel(s0, s1, s2, s3, b1, b2, b3, wide, tall):
    def put(slot, rows):
        wide[pl.ds(row_offset(slot), 32), :] = rows

    for k, part in enumerate((s0, s1, s2, s3)):
        put(k, part[...])
    for g, part in enumerate((b1, b2, b3)):
        for k in range(4):
            put(4 * (g + 1) + k, part[32 * k : 32 * k + 32, :])
    tall[...] = wide[...].T


def gather_kernel(counts, *refs):
    parts, (sums, t_a, t_b, held, sems) = refs[:6], refs[6:]

    def fetch(r):
        rows = pl.ds(128 * r, 128)
        return pltpu.make_async_copy(counts.at[rows, :], held.at[r % 4], sems.at[r % 4])

    for r in range(4):
        fetch(r).start()
    for t, cols in zip((t_a, t_b), HALVES):
        for p, part in enumerate(parts):
            t[64 * p : 64 * p + 64, :] = part[:, cols]
    for r in range(ROWS // 128):
        fetch(r).wait()
        sums[r : r + 1, :] = to_lanes(jnp.sum(held[r % 4].astype(F32), axis=1, keepdims=True))
        if r + 4 < ROWS // 128:
            fetch(r + 4).start()


def join_kernel(low, high, *outs):
    for out, cols in zip(outs, HALVES):
        out[:32, :] = low[:, cols]
        out[32:, :] = high[:, cols]


def far_kernel(*refs):
    (mine_a, theirs_a, mine_b, theirs_b), (low, high) = refs[:4], refs[4:]
    for mine, theirs, cols in ((mine_a, theirs_a, HALVES[0]), (mine_b, theirs_b, HALVES[1])):
        both = (mine[...].astype(F32) + theirs[...].astype(F32)).astype(BF16)
        low[:, cols] = both[:32]
        high[:, cols] = both[32:]


def pair_kernel(mine, theirs_down, theirs_up, low, high, up, down):
    up[:32, :] = (mine[128:160, :].astype(F32) + theirs_up[:32, :].astype(F32) + low[...].astype(F32)).astype(BF16)
    up[32:, :] = (mine[160:, :].astype(F32) + theirs_up[32:, :].astype(F32)).astype(BF16)
    down[:32, :] = (mine[64:96, :].astype(F32) + theirs_down[:32, :].astype(F32)).astype(BF16)
    down[32:, :] = (
        mine[96:128, :].astype(F32) + theirs_down[32:, :].astype(F32) + high[...].astype(F32)
    ).astype(BF16)


def final_kernel(mine, theirs, up, down, out):
    parts = (mine, theirs, up, down)
    out[...] = sum(p[:64, :].astype(F32) for p in parts).astype(BF16)


def softmax_kernel(near, s, mine, theirs, w, stats, tokens, kept, sem, ring=None, sems=None):
    def spill(r):
        return pltpu.make_async_copy(ring.at[r % 4], w.at[pl.ds(128 * r, 128), :], sems.at[r % 4])

    tokens[384:448, :] = mine[...]
    tokens[448:, :] = theirs[...]
    keep = pltpu.make_async_copy(tokens, kept, sem)
    keep.start()
    for r in range(ROWS // 128):
        rows = slice(128 * r, 128 * r + 128)
        logits = jnp.dot(s[rows, :], tokens[...], preferred_element_type=F32)
        top = jnp.max(logits, axis=1, keepdims=True)
        e = jnp.exp(logits - top)
        if ring is None:
            w[rows, :] = e
        else:
            if r >= 4:
                spill(r - 4).wait()
            ring[r % 4] = e
            spill(r).start()
        stats[r : r + 1, :] = to_lanes(top)
        stats[r + 8 : r + 9, :] = to_lanes(jnp.sum(e, axis=1, keepdims=True))
    if ring is not None:
        for r in range(ROWS // 128 - 4, ROWS // 128):
            spill(r).wait()
    keep.wait()


def dlogits_kernel(cols, w, counts, factor, s, dl, mine, theirs):
    for r in range(ROWS // 128):
        rows = slice(128 * r, 128 * r + 128)
        f = to_column(factor[r : r + 1, :])
        dl[rows, :] = (counts[rows, cols].astype(F32) - w[rows, :] * f).astype(BF16)
    out = jnp.dot(s[384:, :], dl[...], preferred_element_type=F32).astype(BF16)
    mine[...] = out[:64]
    theirs[...] = out[64:]


def tok_kernel(s, dl_a, dl_b, mine, *theirs):
    for dl, cols in zip((dl_a, dl_b), HALVES):
        out = jnp.dot(s[:384, :], dl[...], preferred_element_type=F32).astype(BF16)
        for b in range(3):
            rows = slice(64 * b, 64 * b + 64)
            mine[rows, cols] = out[128 * b : 128 * b + 64]
            theirs[b][:, cols] = out[128 * b + 64 : 128 * b + 128]


def state_kernel(t_a, t_b, dl_a, dl_b, out, acc):
    dims = (((1,), (1,)), ((), ()))
    offsets = [row_offset(slot) for slot in range(16)]
    for q in range(4):
        rows = slice(256 * q, 256 * q + 256)
        one = lax.dot_general(t_a[...], dl_a[rows, :], dims, preferred_element_type=F32)
        two = lax.dot_general(t_b[...], dl_b[rows, :], dims, preferred_element_type=F32)
        acc[...] = one + two
        for r in range(16):
            part = acc[pl.ds(offsets[r], 32), :]
            out[32 * r : 32 * r + 32, rows] = part.astype(BF16)


def combine(parts):
    tops = [p[:8] for p in parts]
    top = tops[0]
    for t in tops[1:]:
        top = jnp.maximum(top, t)
    total = sum(p[8:16] * jnp.exp(t - top) for p, t in zip(parts, tops))
    return jnp.concatenate([top, total, sum(p[16:] for p in parts)], axis=0)


def add(*parts):
    return sum(p.astype(F32) for p in parts).astype(BF16)


def body(state_emb, tok_emb, counts):
    own = tok_emb.T

    t2, t4 = x_shift(own, 1), x_shift(own, -1)
    s0 = state_emb.T
    first_parts = [s0] + [shift(s0, 0, k) for k in (1, 2, 3)]
    block = jnp.concatenate(first_parts, axis=0)
    later = [shift(block, 1, k) for k in (1, 2, 3)]
    t1 = core_swap(own)
    t2, t4 = run(hold_kernel, [((64, COLS), BF16)] * 2, t2, t4, wait=(later[0], later[2], t1))

    row_counts, *near = run(
        gather_kernel,
        [((8, 128), F32)] + [((E, HALF), BF16)] * 2,
        counts,
        own,
        t1,
        t2,
        core_swap(t2),
        t4,
        core_swap(t4),
        hbm=1,
        flops=GATHER,
        scratch_shapes=[pltpu.VMEM((4, 128, COLS), BF16), pltpu.SemaphoreType.DMA((4,))],
    )
    wide, tall = run(
        assemble_kernel, [((E, ROWS), BF16), ((ROWS, E), BF16)], *first_parts, *later, wait=(row_counts,)
    )
    mine = run(
        join_kernel,
        [((64, HALF), BF16)] * 2,
        x_shift(t2[:32], 1),
        x_shift(t4[32:], -1),
        wait=(row_counts, wide),
    )
    weights, stats, tokens = [], [], []
    ring = [pltpu.VMEM((4, 128, HALF), F32), pltpu.SemaphoreType.DMA((4,))]
    for t, far in zip(near, mine):
        w, st, _, tk = run(
            softmax_kernel,
            [
                ((ROWS, HALF), F32, HBM) if weights else ((ROWS, HALF), F32),
                ((16, 128), F32),
                ((E, HALF), BF16),
                ((E, HALF), BF16, HBM),
            ],
            t,
            tall,
            far,
            core_swap(far),
            wait=weights,
            flops=2 * ROWS * E * HALF,
            input_output_aliases={0: 2},
            limit=12 if weights else 8,
            scratch_shapes=[pltpu.SemaphoreType.DMA] + (ring if weights else []),
        )
        weights.append(w)
        stats.append(st)
        tokens.append(tk)

    none = jnp.zeros((8, 128), F32)
    total = combine(
        [jnp.concatenate([stats[0], row_counts], axis=0), jnp.concatenate([stats[1], none], axis=0)]
    )
    for stage in range(2):
        total = combine([total] + [shift(total, stage, k) for k in (1, 2, 3)])
    scale = total[16:] / total[8:16]

    dls, sums = [], []
    for w, st, cols in zip(weights, stats, HALVES):
        dl, mine, theirs = run(
            functools.partial(dlogits_kernel, cols),
            [((ROWS, HALF), BF16), ((64, HALF), BF16), ((64, HALF), BF16)],
            w,
            counts,
            jnp.exp(st[:8] - total[:8]) * scale,
            wide,
            wait=dls,
            flops=2 * ROWS * 256 * HALF,
        )
        dls.append(dl)
        sums += [mine, core_swap(theirs)]

    low, high = run(far_kernel, [((32, COLS), BF16)] * 2, *sums)
    from_low, from_high = x_shift(low, 1), x_shift(high, -1)
    mine, *theirs = run(
        tok_kernel,
        [((192, COLS), BF16)] + [((64, COLS), BF16)] * 3,
        wide,
        *dls,
        wait=(low,),
        flops=2 * ROWS * 384 * COLS,
    )
    theirs = [core_swap(t) for t in theirs]
    up, down = run(
        pair_kernel, [((64, COLS), BF16)] * 2, mine, theirs[1], theirs[2], from_low, from_high
    )
    from_up, from_down = x_shift(up, 1), x_shift(down, -1)
    (grad_tok,) = run(final_kernel, [((64, COLS), BF16)], mine, theirs[0], from_up, from_down)

    (g,) = run(
        state_kernel,
        [((E, ROWS), BF16)],
        *tokens,
        *dls,
        wait=(mine,),
        flops=2 * ROWS * E * COLS,
        scratch_shapes=[pltpu.VMEM((E, 256), F32)],
    )
    g = add(g[:128], *[shift(g[128 * k : 128 * k + 128], 1, -k) for k in (1, 2, 3)])
    grad_state = add(g[:32], *[shift(g[32 * k : 32 * k + 32], 0, -k) for k in (1, 2, 3)])
    return grad_state.T, grad_tok.T


def solution(mesh):
    return jax.shard_map(
        body,
        mesh=mesh,
        in_specs=(P("state", "vocab"), P("vocab", "state"), P("state", "vocab")),
        out_specs=(P("state", "vocab"), P("vocab", "state")),
        check_vma=False,
    )
```

```python
import functools

import jax
import jax.numpy as jnp
from jax import lax
from jax.experimental import pallas as pl
from jax.experimental.pallas import tpu as pltpu
from jax.sharding import PartitionSpec as P

F32 = jnp.float32
BF16 = jnp.bfloat16
VMEM = pltpu.MemorySpace.VMEM
SMEM = pltpu.MemorySpace.SMEM
HBM = pltpu.MemorySpace.HBM

E = 512
ROWS = 1024
COLS = 4864
HALF = COLS // 2
HALVES = (slice(0, HALF), slice(HALF, COLS))
NX, NY, NZ = 4, 4, 4
GATHER = 2**31


def core_swap(a):
    return lax.ppermute(a, "state", [(i, i ^ 1) for i in range(8)])


def x_shift(a, step):
    return lax.ppermute(a, "state", [(i, (i + 2 * step) % 8) for i in range(8)])


def shift(a, stage, step):
    perm = []
    for i in range(8):
        for j in range(16):
            z, y = divmod(j, NY)
            if (i % 2 + stage) % 2 == 0:
                y = (y + step) % NY
            else:
                z = (z + step) % NZ
            perm.append((i * 16 + j, i * 16 + z * NY + y))
    return lax.ppermute(a, ("state", "vocab"), perm)


def run(kernel, outs, *ins, flops=64, smem=0, hbm=0, wait=(), limit=8, **kw):
    plain = smem + hbm
    vmem = pl.BlockSpec(memory_space=VMEM)
    anywhere = pl.BlockSpec(memory_space=pl.ANY)
    specs = [pl.BlockSpec(memory_space=SMEM)] * smem + [pl.BlockSpec(memory_space=HBM)] * hbm + [vmem] * (len(ins) - plain)
    args = list(ins[:smem]) + [pltpu.with_memory_space_constraint(a, HBM) for a in ins[smem:plain]]
    args += [pltpu.with_memory_space_constraint(a, VMEM) for a in ins[plain:]]

    def wrapped(*refs):
        kernel(*refs[: len(ins)], *refs[len(ins) + len(wait) :])

    return pl.pallas_call(
        wrapped,
        out_shape=tuple((space[0] if space else VMEM)(shape, dtype) for shape, dtype, *space in outs),
        in_specs=specs + [anywhere] * len(wait),
        out_specs=tuple(pl.BlockSpec(memory_space=o[2]) if o[2:] else vmem for o in outs),
        compiler_params=pltpu.CompilerParams(vmem_limit_bytes=limit * 2**20),
        cost_estimate=pl.CostEstimate(flops=flops, bytes_accessed=64, transcendentals=0),
        **kw,
    )(*args, *wait)


def eye():
    rows = lax.broadcasted_iota(jnp.int32, (128, 128), 0)
    return rows == lax.broadcasted_iota(jnp.int32, (128, 128), 1)


def to_lanes(column):
    return jnp.sum(jnp.where(eye(), jnp.broadcast_to(column, (128, 128)), 0.0), axis=0, keepdims=True)


def to_column(lanes):
    return jnp.sum(jnp.where(eye(), jnp.broadcast_to(lanes, (128, 128)), 0.0), axis=1, keepdims=True)


def hold_kernel(*refs):
    for a, out in zip(refs[:2], refs[2:]):
        out[...] = a[...]


def row_offset(slot):
    i, j = lax.axis_index("state"), lax.axis_index("vocab")
    x, c = lax.div(i, 2), lax.rem(i, 2)
    z, y = lax.div(j, NY), lax.rem(j, NY)
    b, a = divmod(slot, 4)
    y = lax.rem(y + 4 - jnp.where(c == 0, a, b), 4)
    z = lax.rem(z + 4 - jnp.where(c == 0, b, a), 4)
    k = z * NY + y
    owner = lax.div(k, 2)
    ahead = lax.rem(lax.div(owner, 2) + 4 - x, 4)
    place = jnp.where(ahead == 0, 0, jnp.where(ahead == 3, 1, jnp.where(ahead == 1, 2, 3)))
    other = jnp.where(lax.rem(owner, 2) == c, 0, 64)
    return pl.multiple_of(128 * place + other + 32 * lax.rem(k, 2), 32)


def assemble_kernel(s0, s1, s2, s3, b1, b2, b3, wide, tall):
    def put(slot, rows):
        wide[pl.ds(row_offset(slot), 32), :] = rows

    for k, part in enumerate((s0, s1, s2, s3)):
        put(k, part[...])
    for g, part in enumerate((b1, b2, b3)):
        for k in range(4):
            put(4 * (g + 1) + k, part[32 * k : 32 * k + 32, :])
    tall[...] = wide[...].T


def gather_kernel(counts, *refs):
    parts, (sums, t_a, t_b, held, sems) = refs[:6], refs[6:]

    def fetch(r):
        rows = pl.ds(128 * r, 128)
        return pltpu.make_async_copy(counts.at[rows, :], held.at[r % 4], sems.at[r % 4])

    for r in range(4):
        fetch(r).start()
    for t, cols in zip((t_a, t_b), HALVES):
        for p, part in enumerate(parts):
            t[64 * p : 64 * p + 64, :] = part[:, cols]
    for r in range(ROWS // 128):
        fetch(r).wait()
        sums[r : r + 1, :] = to_lanes(jnp.sum(held[r % 4].astype(F32), axis=1, keepdims=True))
        if r + 4 < ROWS // 128:
            fetch(r + 4).start()


def join_kernel(low, high, *outs):
    for out, cols in zip(outs, HALVES):
        out[:32, :] = low[:, cols]
        out[32:, :] = high[:, cols]


def far_kernel(*refs):
    (mine_a, theirs_a, mine_b, theirs_b), (low, high) = refs[:4], refs[4:]
    for mine, theirs, cols in ((mine_a, theirs_a, HALVES[0]), (mine_b, theirs_b, HALVES[1])):
        both = (mine[...].astype(F32) + theirs[...].astype(F32)).astype(BF16)
        low[:, cols] = both[:32]
        high[:, cols] = both[32:]


def pair_kernel(mine, theirs_down, theirs_up, low, high, up, down):
    up[:32, :] = (mine[128:160, :].astype(F32) + theirs_up[:32, :].astype(F32) + low[...].astype(F32)).astype(BF16)
    up[32:, :] = (mine[160:, :].astype(F32) + theirs_up[32:, :].astype(F32)).astype(BF16)
    down[:32, :] = (mine[64:96, :].astype(F32) + theirs_down[:32, :].astype(F32)).astype(BF16)
    down[32:, :] = (
        mine[96:128, :].astype(F32) + theirs_down[32:, :].astype(F32) + high[...].astype(F32)
    ).astype(BF16)


def final_kernel(mine, theirs, up, down, out, held, sems):
    copies = []
    for n, rows in enumerate((slice(0, 32), slice(32, 64))):
        held[rows, :] = sum(p[rows, :].astype(F32) for p in (mine, theirs, up, down)).astype(BF16)
        copies.append(pltpu.make_async_copy(held.at[rows, :], out.at[rows, :], sems.at[n]))
        copies[n].start()
    for copy in copies:
        copy.wait()


def softmax_kernel(spilled, near, s, mine, theirs, w_top, w_low, stats, tokens, kept, sem, *spill):
    tokens[384:448, :] = mine[...]
    tokens[448:, :] = theirs[...]
    keep = pltpu.make_async_copy(tokens, kept, sem)
    keep.start()
    copies = []
    for r in range(ROWS // 128):
        rows = slice(128 * r, 128 * r + 128)
        logits = jnp.dot(s[rows, :], tokens[...], preferred_element_type=F32)
        top = jnp.max(logits, axis=1, keepdims=True)
        e = jnp.exp(logits - top)
        if r >= 4:
            w_low[128 * r - 512 : 128 * r - 384, :] = e
        elif spilled:
            held, sems = spill
            held[rows, :] = e
            copies.append(pltpu.make_async_copy(held.at[rows, :], w_top.at[rows, :], sems.at[r]))
            copies[r].start()
        else:
            w_top[rows, :] = e
        stats[r : r + 1, :] = to_lanes(top)
        stats[r + 8 : r + 9, :] = to_lanes(jnp.sum(e, axis=1, keepdims=True))
    for copy in copies + [keep]:
        copy.wait()


def dlogits_kernel(cols, w_top, w_low, counts, factor, s, dl, mine, theirs):
    for r in range(ROWS // 128):
        rows = slice(128 * r, 128 * r + 128)
        f = to_column(factor[r : r + 1, :])
        w = w_top[rows, :] if r < 4 else w_low[128 * r - 512 : 128 * r - 384, :]
        dl[rows, :] = (counts[rows, cols].astype(F32) - w * f).astype(BF16)
    out = jnp.dot(s[384:, :], dl[...], preferred_element_type=F32).astype(BF16)
    mine[...] = out[:64]
    theirs[...] = out[64:]


def tok_kernel(s, dl_a, dl_b, mine, *theirs):
    for dl, cols in zip((dl_a, dl_b), HALVES):
        out = jnp.dot(s[:384, :], dl[...], preferred_element_type=F32).astype(BF16)
        for b in range(3):
            rows = slice(64 * b, 64 * b + 64)
            mine[rows, cols] = out[128 * b : 128 * b + 64]
            theirs[b][:, cols] = out[128 * b + 64 : 128 * b + 128]


def state_kernel(t_a, t_b, dl_a, dl_b, out, acc):
    dims = (((1,), (1,)), ((), ()))
    offsets = [row_offset(slot) for slot in range(16)]
    for q in range(4):
        rows = slice(256 * q, 256 * q + 256)
        one = lax.dot_general(t_a[...], dl_a[rows, :], dims, preferred_element_type=F32)
        two = lax.dot_general(t_b[...], dl_b[rows, :], dims, preferred_element_type=F32)
        acc[...] = one + two
        for r in range(16):
            part = acc[pl.ds(offsets[r], 32), :]
            out[32 * r : 32 * r + 32, rows] = part.astype(BF16)


def combine(parts):
    tops = [p[:8] for p in parts]
    top = tops[0]
    for t in tops[1:]:
        top = jnp.maximum(top, t)
    total = sum(p[8:16] * jnp.exp(t - top) for p, t in zip(parts, tops))
    return jnp.concatenate([top, total, sum(p[16:] for p in parts)], axis=0)


def add(*parts):
    return sum(p.astype(F32) for p in parts).astype(BF16)


def body(state_emb, tok_emb, counts):
    own = tok_emb.T

    t2, t4 = x_shift(own, 1), x_shift(own, -1)
    s0 = state_emb.T
    first_parts = [s0] + [shift(s0, 0, k) for k in (1, 2, 3)]
    block = jnp.concatenate(first_parts, axis=0)
    later = [shift(block, 1, k) for k in (1, 2, 3)]
    t1 = core_swap(own)
    t2, t4 = run(hold_kernel, [((64, COLS), BF16)] * 2, t2, t4, wait=(later[0], later[2], t1))

    row_counts, *near = run(
        gather_kernel,
        [((8, 128), F32)] + [((E, HALF), BF16)] * 2,
        counts,
        own,
        t1,
        t2,
        core_swap(t2),
        t4,
        core_swap(t4),
        hbm=1,
        flops=GATHER,
        scratch_shapes=[pltpu.VMEM((4, 128, COLS), BF16), pltpu.SemaphoreType.DMA((4,))],
    )
    wide, tall = run(
        assemble_kernel, [((E, ROWS), BF16), ((ROWS, E), BF16)], *first_parts, *later, wait=(row_counts,)
    )
    mine = run(
        join_kernel,
        [((64, HALF), BF16)] * 2,
        x_shift(t2[:32], 1),
        x_shift(t4[32:], -1),
        wait=(row_counts, wide),
    )
    weights, stats, tokens = [], [], []
    for spilled, (t, far) in enumerate(zip(near, mine)):
        spill = [pltpu.VMEM((ROWS // 2, HALF), F32), pltpu.SemaphoreType.DMA((4,))]
        top, low, st, _, tk = run(
            functools.partial(softmax_kernel, spilled),
            [
                ((ROWS // 2, HALF), F32, HBM) if spilled else ((ROWS // 2, HALF), F32),
                ((ROWS // 2, HALF), F32),
                ((16, 128), F32),
                ((E, HALF), BF16),
                ((E, HALF), BF16, HBM),
            ],
            t,
            tall,
            far,
            core_swap(far),
            wait=weights[0] if spilled else (),
            flops=2 * ROWS * E * HALF,
            input_output_aliases={0: 3},
            limit=12 if spilled else 8,
            scratch_shapes=[pltpu.SemaphoreType.DMA] + (spill if spilled else []),
        )
        weights.append((top, low))
        stats.append(st)
        tokens.append(tk)

    none = jnp.zeros((8, 128), F32)
    total = combine(
        [jnp.concatenate([stats[0], row_counts], axis=0), jnp.concatenate([stats[1], none], axis=0)]
    )
    for stage in range(2):
        total = combine([total] + [shift(total, stage, k) for k in (1, 2, 3)])
    scale = total[16:] / total[8:16]

    dls, sums = [], []
    for w, st, cols in zip(weights, stats, HALVES):
        dl, mine, theirs = run(
            functools.partial(dlogits_kernel, cols),
            [((ROWS, HALF), BF16), ((64, HALF), BF16), ((64, HALF), BF16)],
            *w,
            counts,
            jnp.exp(st[:8] - total[:8]) * scale,
            wide,
            wait=dls,
            flops=2 * ROWS * 256 * HALF,
        )
        dls.append(dl)
        sums += [mine, core_swap(theirs)]

    low, high = run(far_kernel, [((32, COLS), BF16)] * 2, *sums)
    from_low, from_high = x_shift(low, 1), x_shift(high, -1)
    mine, *theirs = run(
        tok_kernel,
        [((192, COLS), BF16)] + [((64, COLS), BF16)] * 3,
        wide,
        *dls,
        wait=(low,),
        flops=2 * ROWS * 384 * COLS,
    )
    theirs = [core_swap(t) for t in theirs]
    up, down = run(
        pair_kernel,
        [((64, COLS), BF16)] * 2,
        mine,
        theirs[1],
        theirs[2],
        from_low,
        from_high,
        wait=(theirs[0],),
    )
    from_up, from_down = x_shift(up, 1), x_shift(down, -1)
    (grad_tok,) = run(
        final_kernel,
        [((64, COLS), BF16, HBM)],
        mine,
        theirs[0],
        from_up,
        from_down,
        scratch_shapes=[pltpu.VMEM((64, COLS), BF16), pltpu.SemaphoreType.DMA((2,))],
    )

    (g,) = run(
        state_kernel,
        [((E, ROWS), BF16)],
        *tokens,
        *dls,
        wait=(mine,),
        flops=2 * ROWS * E * COLS,
        scratch_shapes=[pltpu.VMEM((E, 256), F32)],
    )
    g = add(g[:128], *[shift(g[128 * k : 128 * k + 128], 1, -k) for k in (1, 2, 3)])
    grad_state = add(g[:32], *[shift(g[32 * k : 32 * k + 32], 0, -k) for k in (1, 2, 3)])
    return grad_state.T, grad_tok.T


def solution(mesh):
    return jax.shard_map(
        body,
        mesh=mesh,
        in_specs=(P("state", "vocab"), P("vocab", "state"), P("state", "vocab")),
        out_specs=(P("state", "vocab"), P("vocab", "state")),
        check_vma=False,
    )
```

```python
import functools

import jax
import jax.numpy as jnp
from jax import lax
from jax.experimental import pallas as pl
from jax.experimental.pallas import tpu as pltpu
from jax.sharding import PartitionSpec as P

F32 = jnp.float32
BF16 = jnp.bfloat16
VMEM = pltpu.MemorySpace.VMEM
SMEM = pltpu.MemorySpace.SMEM
HBM = pltpu.MemorySpace.HBM

E = 512
ROWS = 1024
COLS = 4864
HALF = COLS // 2
HALVES = (slice(0, HALF), slice(HALF, COLS))
NX, NY, NZ = 4, 4, 4
GATHER = 2**31


def core_swap(a):
    return lax.ppermute(a, "state", [(i, i ^ 1) for i in range(8)])


def x_shift(a, step):
    return lax.ppermute(a, "state", [(i, (i + 2 * step) % 8) for i in range(8)])


def shift(a, stage, step):
    perm = []
    for i in range(8):
        for j in range(16):
            z, y = divmod(j, NY)
            if (i % 2 + stage) % 2 == 0:
                y = (y + step) % NY
            else:
                z = (z + step) % NZ
            perm.append((i * 16 + j, i * 16 + z * NY + y))
    return lax.ppermute(a, ("state", "vocab"), perm)


def run(kernel, outs, *ins, flops=64, smem=0, hbm=0, wait=(), limit=8, **kw):
    plain = smem + hbm
    vmem = pl.BlockSpec(memory_space=VMEM)
    anywhere = pl.BlockSpec(memory_space=pl.ANY)
    specs = [pl.BlockSpec(memory_space=SMEM)] * smem + [pl.BlockSpec(memory_space=HBM)] * hbm + [vmem] * (len(ins) - plain)
    args = list(ins[:smem]) + [pltpu.with_memory_space_constraint(a, HBM) for a in ins[smem:plain]]
    args += [pltpu.with_memory_space_constraint(a, VMEM) for a in ins[plain:]]

    def wrapped(*refs):
        kernel(*refs[: len(ins)], *refs[len(ins) + len(wait) :])

    return pl.pallas_call(
        wrapped,
        out_shape=tuple((space[0] if space else VMEM)(shape, dtype) for shape, dtype, *space in outs),
        in_specs=specs + [anywhere] * len(wait),
        out_specs=tuple(pl.BlockSpec(memory_space=o[2]) if o[2:] else vmem for o in outs),
        compiler_params=pltpu.CompilerParams(vmem_limit_bytes=limit * 2**20),
        cost_estimate=pl.CostEstimate(flops=flops, bytes_accessed=64, transcendentals=0),
        **kw,
    )(*args, *wait)


def eye():
    rows = lax.broadcasted_iota(jnp.int32, (128, 128), 0)
    return rows == lax.broadcasted_iota(jnp.int32, (128, 128), 1)


def to_lanes(column):
    return jnp.sum(jnp.where(eye(), jnp.broadcast_to(column, (128, 128)), 0.0), axis=0, keepdims=True)


def to_column(lanes):
    return jnp.sum(jnp.where(eye(), jnp.broadcast_to(lanes, (128, 128)), 0.0), axis=1, keepdims=True)


def hold_kernel(*refs):
    for a, out in zip(refs[:2], refs[2:]):
        out[...] = a[...]


def row_offset(slot):
    i, j = lax.axis_index("state"), lax.axis_index("vocab")
    x, c = lax.div(i, 2), lax.rem(i, 2)
    z, y = lax.div(j, NY), lax.rem(j, NY)
    b, a = divmod(slot, 4)
    y = lax.rem(y + 4 - jnp.where(c == 0, a, b), 4)
    z = lax.rem(z + 4 - jnp.where(c == 0, b, a), 4)
    k = z * NY + y
    owner = lax.div(k, 2)
    ahead = lax.rem(lax.div(owner, 2) + 4 - x, 4)
    place = jnp.where(ahead == 0, 0, jnp.where(ahead == 3, 1, jnp.where(ahead == 1, 2, 3)))
    other = jnp.where(lax.rem(owner, 2) == c, 0, 64)
    return pl.multiple_of(128 * place + other + 32 * lax.rem(k, 2), 32)


def assemble_kernel(s0, s1, s2, s3, b1, b2, b3, wide, tall):
    def put(slot, rows):
        wide[pl.ds(row_offset(slot), 32), :] = rows

    for k, part in enumerate((s0, s1, s2, s3)):
        put(k, part[...])
    for g, part in enumerate((b1, b2, b3)):
        for k in range(4):
            put(4 * (g + 1) + k, part[32 * k : 32 * k + 32, :])
    tall[...] = wide[...].T


def gather_kernel(counts, *refs):
    parts, (sums, t_a, t_b, held, sems) = refs[:6], refs[6:]

    def fetch(r):
        rows = pl.ds(128 * r, 128)
        return pltpu.make_async_copy(counts.at[rows, :], held.at[r % 4], sems.at[r % 4])

    for r in range(4):
        fetch(r).start()
    for t, cols in zip((t_a, t_b), HALVES):
        for p, part in enumerate(parts):
            t[64 * p : 64 * p + 64, :] = part[:, cols]
    for r in range(ROWS // 128):
        fetch(r).wait()
        sums[r : r + 1, :] = to_lanes(jnp.sum(held[r % 4].astype(F32), axis=1, keepdims=True))
        if r + 4 < ROWS // 128:
            fetch(r + 4).start()


def join_kernel(low, high, *outs):
    for out, cols in zip(outs, HALVES):
        out[:32, :] = low[:, cols]
        out[32:, :] = high[:, cols]


def far_kernel(*refs):
    (mine_a, theirs_a, mine_b, theirs_b), (low, high) = refs[:4], refs[4:]
    for mine, theirs, cols in ((mine_a, theirs_a, HALVES[0]), (mine_b, theirs_b, HALVES[1])):
        both = (mine[...].astype(F32) + theirs[...].astype(F32)).astype(BF16)
        low[:, cols] = both[:32]
        high[:, cols] = both[32:]


def pair_kernel(mine, theirs_down, theirs_up, low, high, up, down):
    up[:32, :] = (mine[128:160, :].astype(F32) + theirs_up[:32, :].astype(F32) + low[...].astype(F32)).astype(BF16)
    up[32:, :] = (mine[160:, :].astype(F32) + theirs_up[32:, :].astype(F32)).astype(BF16)
    down[:32, :] = (mine[64:96, :].astype(F32) + theirs_down[:32, :].astype(F32)).astype(BF16)
    down[32:, :] = (
        mine[96:128, :].astype(F32) + theirs_down[32:, :].astype(F32) + high[...].astype(F32)
    ).astype(BF16)


def final_kernel(mine, theirs, up, down, out, held, sems):
    copies = []
    for n, rows in enumerate((slice(0, 32), slice(32, 64))):
        held[rows, :] = sum(p[rows, :].astype(F32) for p in (mine, theirs, up, down)).astype(BF16)
        copies.append(pltpu.make_async_copy(held.at[rows, :], out.at[rows, :], sems.at[n]))
        copies[n].start()
    for copy in copies:
        copy.wait()


def softmax_kernel(spilled, near, s, mine, theirs, w_top, w_low, stats, tokens, kept, sem, *spill):
    tokens[384:448, :] = mine[...]
    tokens[448:, :] = theirs[...]
    keep = pltpu.make_async_copy(tokens, kept, sem)
    keep.start()
    copies = []
    for r in range(ROWS // 128):
        rows = slice(128 * r, 128 * r + 128)
        logits = jnp.dot(s[rows, :], tokens[...], preferred_element_type=F32)
        top = jnp.max(logits, axis=1, keepdims=True)
        e = jnp.exp(logits - top)
        if r >= 4:
            w_low[128 * r - 512 : 128 * r - 384, :] = e
        elif spilled:
            held, sems = spill
            held[rows, :] = e
            copies.append(pltpu.make_async_copy(held.at[rows, :], w_top.at[rows, :], sems.at[r]))
            copies[r].start()
        else:
            w_top[rows, :] = e
        stats[r : r + 1, :] = to_lanes(top)
        stats[r + 8 : r + 9, :] = to_lanes(jnp.sum(e, axis=1, keepdims=True))
    for copy in copies + [keep]:
        copy.wait()


def dlogits_kernel(cols, w_top, w_low, counts, factor, s, dl, mine, theirs):
    for r in range(ROWS // 128):
        rows = slice(128 * r, 128 * r + 128)
        f = to_column(factor[r : r + 1, :])
        w = w_top[rows, :] if r < 4 else w_low[128 * r - 512 : 128 * r - 384, :]
        dl[rows, :] = (counts[rows, cols].astype(F32) - w * f).astype(BF16)
    out = jnp.dot(s[384:, :], dl[...], preferred_element_type=F32).astype(BF16)
    mine[...] = out[:64]
    theirs[...] = out[64:]


def tok_kernel(s, dl_a, dl_b, mine, *theirs):
    for dl, cols in zip((dl_a, dl_b), HALVES):
        out = jnp.dot(s[:384, :], dl[...], preferred_element_type=F32).astype(BF16)
        for b in range(3):
            rows = slice(64 * b, 64 * b + 64)
            mine[rows, cols] = out[128 * b : 128 * b + 64]
            theirs[b][:, cols] = out[128 * b + 64 : 128 * b + 128]


def state_kernel(t_a, t_b, dl_a, dl_b, out, acc):
    dims = (((1,), (1,)), ((), ()))
    offsets = [row_offset(slot) for slot in range(16)]
    for q in range(4):
        rows = slice(256 * q, 256 * q + 256)
        one = lax.dot_general(t_a[...], dl_a[rows, :], dims, preferred_element_type=F32)
        two = lax.dot_general(t_b[...], dl_b[rows, :], dims, preferred_element_type=F32)
        acc[...] = one + two
        for r in range(16):
            part = acc[pl.ds(offsets[r], 32), :]
            out[32 * r : 32 * r + 32, rows] = part.astype(BF16)


def combine(parts):
    tops = [p[:8] for p in parts]
    top = tops[0]
    for t in tops[1:]:
        top = jnp.maximum(top, t)
    total = sum(p[8:16] * jnp.exp(t - top) for p, t in zip(parts, tops))
    return jnp.concatenate([top, total, sum(p[16:] for p in parts)], axis=0)


def add(*parts):
    return sum(p.astype(F32) for p in parts).astype(BF16)


def body(state_emb, tok_emb, counts):
    own = tok_emb.T

    t2, t4 = x_shift(own, 1), x_shift(own, -1)
    s0 = state_emb.T
    first_parts = [s0] + [shift(s0, 0, k) for k in (1, 2, 3)]
    block = jnp.concatenate(first_parts, axis=0)
    later = [shift(block, 1, k) for k in (1, 2, 3)]
    t1 = core_swap(own)
    t2, t4 = run(hold_kernel, [((64, COLS), BF16)] * 2, t2, t4, wait=(later[0], later[2]))

    row_counts, *near = run(
        gather_kernel,
        [((8, 128), F32)] + [((E, HALF), BF16)] * 2,
        counts,
        own,
        t1,
        t2,
        core_swap(t2),
        t4,
        core_swap(t4),
        hbm=1,
        flops=GATHER,
        scratch_shapes=[pltpu.VMEM((4, 128, COLS), BF16), pltpu.SemaphoreType.DMA((4,))],
    )
    wide, tall = run(
        assemble_kernel, [((E, ROWS), BF16), ((ROWS, E), BF16)], *first_parts, *later, wait=(row_counts,)
    )
    mine = run(
        join_kernel,
        [((64, HALF), BF16)] * 2,
        x_shift(t2[:32], 1),
        x_shift(t4[32:], -1),
        wait=(row_counts, wide),
    )
    weights, stats, tokens = [], [], []
    for spilled, (t, far) in enumerate(zip(near, mine)):
        spill = [pltpu.VMEM((ROWS // 2, HALF), F32), pltpu.SemaphoreType.DMA((4,))]
        top, low, st, _, tk = run(
            functools.partial(softmax_kernel, spilled),
            [
                ((ROWS // 2, HALF), F32, HBM) if spilled else ((ROWS // 2, HALF), F32),
                ((ROWS // 2, HALF), F32),
                ((16, 128), F32),
                ((E, HALF), BF16),
                ((E, HALF), BF16, HBM),
            ],
            t,
            tall,
            far,
            core_swap(far),
            wait=weights[0] if spilled else (),
            flops=2 * ROWS * E * HALF,
            input_output_aliases={0: 3},
            limit=12 if spilled else 8,
            scratch_shapes=[pltpu.SemaphoreType.DMA] + (spill if spilled else []),
        )
        weights.append((top, low))
        stats.append(st)
        tokens.append(tk)

    none = jnp.zeros((8, 128), F32)
    total = combine(
        [jnp.concatenate([stats[0], row_counts], axis=0), jnp.concatenate([stats[1], none], axis=0)]
    )
    for stage in range(2):
        total = combine([total] + [shift(total, stage, k) for k in (1, 2, 3)])
    scale = total[16:] / total[8:16]

    dls, sums = [], []
    for w, st, cols in zip(weights, stats, HALVES):
        dl, mine, theirs = run(
            functools.partial(dlogits_kernel, cols),
            [((ROWS, HALF), BF16), ((64, HALF), BF16), ((64, HALF), BF16)],
            *w,
            counts,
            jnp.exp(st[:8] - total[:8]) * scale,
            wide,
            wait=dls,
            flops=2 * ROWS * 256 * HALF,
        )
        dls.append(dl)
        sums += [mine, core_swap(theirs)]

    low, high = run(far_kernel, [((32, COLS), BF16)] * 2, *sums)
    from_low, from_high = x_shift(low, 1), x_shift(high, -1)
    mine, *theirs = run(
        tok_kernel,
        [((192, COLS), BF16)] + [((64, COLS), BF16)] * 3,
        wide,
        *dls,
        wait=(low,),
        flops=2 * ROWS * 384 * COLS,
    )
    theirs = [core_swap(t) for t in theirs]
    up, down = run(
        pair_kernel,
        [((64, COLS), BF16)] * 2,
        mine,
        theirs[1],
        theirs[2],
        from_low,
        from_high,
        wait=(theirs[0],),
    )
    from_up, from_down = x_shift(up, 1), x_shift(down, -1)
    (grad_tok,) = run(
        final_kernel,
        [((64, COLS), BF16, HBM)],
        mine,
        theirs[0],
        from_up,
        from_down,
        scratch_shapes=[pltpu.VMEM((64, COLS), BF16), pltpu.SemaphoreType.DMA((2,))],
    )

    (g,) = run(
        state_kernel,
        [((E, ROWS), BF16)],
        *tokens,
        *dls,
        wait=(mine,),
        flops=2 * ROWS * E * COLS,
        scratch_shapes=[pltpu.VMEM((E, 256), F32)],
    )
    g = add(g[:128], *[shift(g[128 * k : 128 * k + 128], 1, -k) for k in (1, 2, 3)])
    grad_state = add(g[:32], *[shift(g[32 * k : 32 * k + 32], 0, -k) for k in (1, 2, 3)])
    return grad_state.T, grad_tok.T


def solution(mesh):
    return jax.shard_map(
        body,
        mesh=mesh,
        in_specs=(P("state", "vocab"), P("vocab", "state"), P("state", "vocab")),
        out_specs=(P("state", "vocab"), P("vocab", "state")),
        check_vma=False,
    )
```

```python
import functools

import jax
import jax.numpy as jnp
from jax import lax
from jax.experimental import pallas as pl
from jax.experimental.pallas import tpu as pltpu
from jax.sharding import PartitionSpec as P

F32 = jnp.float32
BF16 = jnp.bfloat16
VMEM = pltpu.MemorySpace.VMEM
SMEM = pltpu.MemorySpace.SMEM
HBM = pltpu.MemorySpace.HBM

E = 512
ROWS = 1024
COLS = 4864
HALF = COLS // 2
HALVES = (slice(0, HALF), slice(HALF, COLS))
NX, NY, NZ = 4, 4, 4
GATHER = 2**31


def core_swap(a):
    return lax.ppermute(a, "state", [(i, i ^ 1) for i in range(8)])


def x_shift(a, step):
    return lax.ppermute(a, "state", [(i, (i + 2 * step) % 8) for i in range(8)])


def shift(a, stage, step):
    perm = []
    for i in range(8):
        for j in range(16):
            z, y = divmod(j, NY)
            if (i % 2 + stage) % 2 == 0:
                y = (y + step) % NY
            else:
                z = (z + step) % NZ
            perm.append((i * 16 + j, i * 16 + z * NY + y))
    return lax.ppermute(a, ("state", "vocab"), perm)


def run(kernel, outs, *ins, flops=64, smem=0, hbm=0, wait=(), limit=8, **kw):
    plain = smem + hbm
    vmem = pl.BlockSpec(memory_space=VMEM)
    anywhere = pl.BlockSpec(memory_space=pl.ANY)
    specs = [pl.BlockSpec(memory_space=SMEM)] * smem + [pl.BlockSpec(memory_space=HBM)] * hbm + [vmem] * (len(ins) - plain)
    args = list(ins[:smem]) + [pltpu.with_memory_space_constraint(a, HBM) for a in ins[smem:plain]]
    args += [pltpu.with_memory_space_constraint(a, VMEM) for a in ins[plain:]]

    def wrapped(*refs):
        kernel(*refs[: len(ins)], *refs[len(ins) + len(wait) :])

    return pl.pallas_call(
        wrapped,
        out_shape=tuple((space[0] if space else VMEM)(shape, dtype) for shape, dtype, *space in outs),
        in_specs=specs + [anywhere] * len(wait),
        out_specs=tuple(pl.BlockSpec(memory_space=o[2]) if o[2:] else vmem for o in outs),
        compiler_params=pltpu.CompilerParams(vmem_limit_bytes=limit * 2**20),
        cost_estimate=pl.CostEstimate(flops=flops, bytes_accessed=64, transcendentals=0),
        **kw,
    )(*args, *wait)


def eye():
    rows = lax.broadcasted_iota(jnp.int32, (128, 128), 0)
    return rows == lax.broadcasted_iota(jnp.int32, (128, 128), 1)


def to_lanes(column):
    return jnp.sum(jnp.where(eye(), jnp.broadcast_to(column, (128, 128)), 0.0), axis=0, keepdims=True)


def to_column(lanes):
    return jnp.sum(jnp.where(eye(), jnp.broadcast_to(lanes, (128, 128)), 0.0), axis=1, keepdims=True)


def hold_kernel(*refs):
    for a, out in zip(refs[:2], refs[2:]):
        out[...] = a[...]


def row_offset(slot):
    i, j = lax.axis_index("state"), lax.axis_index("vocab")
    x, c = lax.div(i, 2), lax.rem(i, 2)
    z, y = lax.div(j, NY), lax.rem(j, NY)
    b, a = divmod(slot, 4)
    y = lax.rem(y + 4 - jnp.where(c == 0, a, b), 4)
    z = lax.rem(z + 4 - jnp.where(c == 0, b, a), 4)
    k = z * NY + y
    owner = lax.div(k, 2)
    ahead = lax.rem(lax.div(owner, 2) + 4 - x, 4)
    place = jnp.where(ahead == 0, 0, jnp.where(ahead == 3, 1, jnp.where(ahead == 1, 2, 3)))
    other = jnp.where(lax.rem(owner, 2) == c, 0, 64)
    return pl.multiple_of(128 * place + other + 32 * lax.rem(k, 2), 32)


def assemble_kernel(s0, s1, s2, s3, b1, b2, b3, wide, tall):
    def put(slot, rows):
        wide[pl.ds(row_offset(slot), 32), :] = rows

    for k, part in enumerate((s0, s1, s2, s3)):
        put(k, part[...])
    for g, part in enumerate((b1, b2, b3)):
        for k in range(4):
            put(4 * (g + 1) + k, part[32 * k : 32 * k + 32, :])
    tall[...] = wide[...].T


def gather_kernel(counts, *refs):
    parts, (sums, t_a, t_b, held, sems) = refs[:6], refs[6:]

    def fetch(r):
        rows = pl.ds(128 * r, 128)
        return pltpu.make_async_copy(counts.at[rows, :], held.at[r % 4], sems.at[r % 4])

    for r in range(4):
        fetch(r).start()
    for t, cols in zip((t_a, t_b), HALVES):
        for p, part in enumerate(parts):
            t[64 * p : 64 * p + 64, :] = part[:, cols]
    for r in range(ROWS // 128):
        fetch(r).wait()
        sums[r : r + 1, :] = to_lanes(jnp.sum(held[r % 4].astype(F32), axis=1, keepdims=True))
        if r + 4 < ROWS // 128:
            fetch(r + 4).start()


def join_kernel(low, high, *outs):
    for out, cols in zip(outs, HALVES):
        out[:32, :] = low[:, cols]
        out[32:, :] = high[:, cols]


def far_kernel(*refs):
    (mine_a, theirs_a, mine_b, theirs_b), (low, high) = refs[:4], refs[4:]
    for mine, theirs, cols in ((mine_a, theirs_a, HALVES[0]), (mine_b, theirs_b, HALVES[1])):
        both = (mine[...].astype(F32) + theirs[...].astype(F32)).astype(BF16)
        low[:, cols] = both[:32]
        high[:, cols] = both[32:]


def pair_kernel(mine, theirs_down, theirs_up, low, high, up, down):
    up[:32, :] = (mine[128:160, :].astype(F32) + theirs_up[:32, :].astype(F32) + low[...].astype(F32)).astype(BF16)
    up[32:, :] = (mine[160:, :].astype(F32) + theirs_up[32:, :].astype(F32)).astype(BF16)
    down[:32, :] = (mine[64:96, :].astype(F32) + theirs_down[:32, :].astype(F32)).astype(BF16)
    down[32:, :] = (
        mine[96:128, :].astype(F32) + theirs_down[32:, :].astype(F32) + high[...].astype(F32)
    ).astype(BF16)


def final_kernel(mine, theirs, up, down, out, held, sems):
    copies = []
    for n, rows in enumerate((slice(0, 32), slice(32, 64))):
        held[rows, :] = sum(p[rows, :].astype(F32) for p in (mine, theirs, up, down)).astype(BF16)
        copies.append(pltpu.make_async_copy(held.at[rows, :], out.at[rows, :], sems.at[n]))
        copies[n].start()
    for copy in copies:
        copy.wait()


def softmax_kernel(spilled, near, s, mine, theirs, w_top, w_low, stats, tokens, kept, sem, *spill):
    tokens[384:448, :] = mine[...]
    tokens[448:, :] = theirs[...]
    keep = pltpu.make_async_copy(tokens, kept, sem)
    keep.start()
    copies = []
    for r in range(ROWS // 128):
        rows = slice(128 * r, 128 * r + 128)
        logits = jnp.dot(s[rows, :], tokens[...], preferred_element_type=F32)
        top = jnp.max(logits, axis=1, keepdims=True)
        e = jnp.exp(logits - top)
        if r >= 4:
            w_low[128 * r - 512 : 128 * r - 384, :] = e
        elif spilled:
            held, sems = spill
            held[rows, :] = e
            copies.append(pltpu.make_async_copy(held.at[rows, :], w_top.at[rows, :], sems.at[r]))
            copies[r].start()
        else:
            w_top[rows, :] = e
        stats[r : r + 1, :] = to_lanes(top)
        stats[r + 8 : r + 9, :] = to_lanes(jnp.sum(e, axis=1, keepdims=True))
    for copy in copies + [keep]:
        copy.wait()


def dlogits_kernel(cols, w_top, w_low, counts, factor, s, dl, mine, theirs):
    for r in range(ROWS // 128):
        rows = slice(128 * r, 128 * r + 128)
        f = to_column(factor[r : r + 1, :])
        w = w_top[rows, :] if r < 4 else w_low[128 * r - 512 : 128 * r - 384, :]
        dl[rows, :] = (counts[rows, cols].astype(F32) - w * f).astype(BF16)
    out = jnp.dot(s[384:, :], dl[...], preferred_element_type=F32).astype(BF16)
    mine[...] = out[:64]
    theirs[...] = out[64:]


def tok_kernel(s, dl_a, dl_b, mine, *theirs):
    for dl, cols in zip((dl_a, dl_b), HALVES):
        out = jnp.dot(s[:384, :], dl[...], preferred_element_type=F32).astype(BF16)
        for b in range(3):
            rows = slice(64 * b, 64 * b + 64)
            mine[rows, cols] = out[128 * b : 128 * b + 64]
            theirs[b][:, cols] = out[128 * b + 64 : 128 * b + 128]


def state_kernel(t_a, t_b, dl_a, dl_b, out, acc):
    dims = (((1,), (1,)), ((), ()))
    offsets = [row_offset(slot) for slot in range(16)]
    for q in range(4):
        rows = slice(256 * q, 256 * q + 256)
        one = lax.dot_general(t_a[...], dl_a[rows, :], dims, preferred_element_type=F32)
        two = lax.dot_general(t_b[...], dl_b[rows, :], dims, preferred_element_type=F32)
        acc[...] = one + two
        for r in range(16):
            part = acc[pl.ds(offsets[r], 32), :]
            out[32 * r : 32 * r + 32, rows] = part.astype(BF16)


def combine(parts):
    tops = [p[:8] for p in parts]
    top = tops[0]
    for t in tops[1:]:
        top = jnp.maximum(top, t)
    total = sum(p[8:16] * jnp.exp(t - top) for p, t in zip(parts, tops))
    return jnp.concatenate([top, total, sum(p[16:] for p in parts)], axis=0)


def add(*parts):
    return sum(p.astype(F32) for p in parts).astype(BF16)


def body(state_emb, tok_emb, counts):
    own = tok_emb.T

    t2, t4 = x_shift(own, 1), x_shift(own, -1)
    s0 = state_emb.T
    first_parts = [s0] + [shift(s0, 0, k) for k in (1, 2, 3)]
    block = jnp.concatenate(first_parts, axis=0)
    later = [shift(block, 1, k) for k in (1, 2, 3)]
    t1 = core_swap(own)
    t2, t4 = run(hold_kernel, [((64, COLS), BF16)] * 2, t2, t4, wait=(later[0],))

    row_counts, *near = run(
        gather_kernel,
        [((8, 128), F32)] + [((E, HALF), BF16)] * 2,
        counts,
        own,
        t1,
        t2,
        core_swap(t2),
        t4,
        core_swap(t4),
        hbm=1,
        flops=GATHER,
        scratch_shapes=[pltpu.VMEM((4, 128, COLS), BF16), pltpu.SemaphoreType.DMA((4,))],
    )
    wide, tall = run(
        assemble_kernel, [((E, ROWS), BF16), ((ROWS, E), BF16)], *first_parts, *later, wait=(row_counts,)
    )
    mine = run(
        join_kernel,
        [((64, HALF), BF16)] * 2,
        x_shift(t2[:32], 1),
        x_shift(t4[32:], -1),
        wait=(row_counts, wide),
    )
    weights, stats, tokens = [], [], []
    for spilled, (t, far) in enumerate(zip(near, mine)):
        spill = [pltpu.VMEM((ROWS // 2, HALF), F32), pltpu.SemaphoreType.DMA((4,))]
        top, low, st, _, tk = run(
            functools.partial(softmax_kernel, spilled),
            [
                ((ROWS // 2, HALF), F32, HBM) if spilled else ((ROWS // 2, HALF), F32),
                ((ROWS // 2, HALF), F32),
                ((16, 128), F32),
                ((E, HALF), BF16),
                ((E, HALF), BF16, HBM),
            ],
            t,
            tall,
            far,
            core_swap(far),
            wait=weights[0] if spilled else (),
            flops=2 * ROWS * E * HALF,
            input_output_aliases={0: 3},
            limit=12 if spilled else 8,
            scratch_shapes=[pltpu.SemaphoreType.DMA] + (spill if spilled else []),
        )
        weights.append((top, low))
        stats.append(st)
        tokens.append(tk)

    none = jnp.zeros((8, 128), F32)
    total = combine(
        [jnp.concatenate([stats[0], row_counts], axis=0), jnp.concatenate([stats[1], none], axis=0)]
    )
    for stage in range(2):
        total = combine([total] + [shift(total, stage, k) for k in (1, 2, 3)])
    scale = total[16:] / total[8:16]

    dls, sums = [], []
    for w, st, cols in zip(weights, stats, HALVES):
        dl, mine, theirs = run(
            functools.partial(dlogits_kernel, cols),
            [((ROWS, HALF), BF16), ((64, HALF), BF16), ((64, HALF), BF16)],
            *w,
            counts,
            jnp.exp(st[:8] - total[:8]) * scale,
            wide,
            wait=dls,
            flops=2 * ROWS * 256 * HALF,
        )
        dls.append(dl)
        sums += [mine, core_swap(theirs)]

    low, high = run(far_kernel, [((32, COLS), BF16)] * 2, *sums)
    from_low, from_high = x_shift(low, 1), x_shift(high, -1)
    mine, *theirs = run(
        tok_kernel,
        [((192, COLS), BF16)] + [((64, COLS), BF16)] * 3,
        wide,
        *dls,
        wait=(low,),
        flops=2 * ROWS * 384 * COLS,
    )
    theirs = [core_swap(t) for t in theirs]
    up, down = run(
        pair_kernel,
        [((64, COLS), BF16)] * 2,
        mine,
        theirs[1],
        theirs[2],
        from_low,
        from_high,
        wait=(theirs[0],),
    )
    from_up, from_down = x_shift(up, 1), x_shift(down, -1)
    (grad_tok,) = run(
        final_kernel,
        [((64, COLS), BF16, HBM)],
        mine,
        theirs[0],
        from_up,
        from_down,
        scratch_shapes=[pltpu.VMEM((64, COLS), BF16), pltpu.SemaphoreType.DMA((2,))],
    )

    (g,) = run(
        state_kernel,
        [((E, ROWS), BF16)],
        *tokens,
        *dls,
        wait=(mine,),
        flops=2 * ROWS * E * COLS,
        scratch_shapes=[pltpu.VMEM((E, 256), F32)],
    )
    g = add(g[:128], *[shift(g[128 * k : 128 * k + 128], 1, -k) for k in (1, 2, 3)])
    grad_state = add(g[:32], *[shift(g[32 * k : 32 * k + 32], 0, -k) for k in (1, 2, 3)])
    return grad_state.T, grad_tok.T


def solution(mesh):
    return jax.shard_map(
        body,
        mesh=mesh,
        in_specs=(P("state", "vocab"), P("vocab", "state"), P("state", "vocab")),
        out_specs=(P("state", "vocab"), P("vocab", "state")),
        check_vma=False,
    )
```
